256 devices in a mesh: oi: 16 (over y, x), oj: 16 (over z, core).
Axes of the slice: x: 4, y: 4, z: 8, core: 2. Of those that a mesh axis runs over, the one named last changes fastest.
Arguments:
- amplitudes: float32 [1024, 128, 128], P(('oi', 'oj')), may hold values from -4 to 4
- integrals: float32 [1024, 128, 128], P(('oi', 'oj')), may hold values from -6 to 6
- pno_energy: float32 [1024, 128], P(('oi', 'oj')), may hold values from 0.3 to 3
- pair_shift: float32 [1024], P(('oi', 'oj')), may hold values from 0.5 to 2
- column_margin: bfloat16 [32768, 128, 128], P(('oi', 'oj')), may hold values from -0.5 to 1.8, as said below
- row_margin: bfloat16 [32768, 128, 128], P(('oi', 'oj')), may hold values from -0.5 to 1.8, as said below
- column_coupling: float32 [32768], P(('oi', 'oj')), may hold values from -0.3 to 0.3
- row_coupling: float32 [32768], P(('oi', 'oj')), may hold values from -0.3 to 0.3
- column_target: int32 [32768], P(('oi', 'oj')), may hold values from 0 to 3
- row_target: int32 [32768], P(('oi', 'oj')), may hold values from 0 to 3
- column_source: int32 [32768], P(('oi', 'oj')), may hold values from 0 to 31
- row_source: int32 [32768], P(('oi', 'oj')), may hold values from 0 to 31
- column_sends: int32 [4096, 2], P(('oi', 'oj')), may hold values from 0 to 3, as said below
- row_sends: int32 [4096, 2], P(('oi', 'oj')), may hold values from 0 to 3, as said below
- term_counts: int32 [256, 2], P(('oi', 'oj')), may hold values from 1 to 128, as said below
Outputs:
- updated: float32 [1024, 128, 128], P(('oi', 'oj'))
- residual: float32 [1024, 128, 128], P(('oi', 'oj'))
The draws below stay inside these ranges and needn't reach their ends.
Inputs may be any that keep to these rules, and one draw needn't show every extreme that they name: `column_margin`: each margin block is a 128 by 128 matrix of rank 128. `row_margin`: each margin block is a 128 by 128 matrix of rank 128. `column_sends`: each row names 2 different local pairs of its device. `row_sends`: each row names 2 different local pairs of its device. `term_counts`: some device has 128 live column terms and some device 128 live row terms.
All inputs are finite; a program needn't handle non-finite values.
Results may differ from the reference program's by a relative error of at most 0.0041.
Values may be sent and summed in bfloat16 or wider, within the bound.
No kernel may reach another device: no remote copies, remote signals or barrier semaphores. Data moves between devices by JAX's collectives and lax.ppermute only.
A program may use at most 128 MiB of HBM per device.

```python
import math
import jax
import jax.numpy as jnp
from jax import lax

PNO = 128
PAIRS_DEV = 4
CAP = 2
TERMS_DEV = 128
ITERS = 2
PAIRS = 1024
TERMS = 32768
N_OI = 16
N_OJ = 16


def margin_draw(key, term_total):
    diag_key, jitter_key = jax.random.split(key, 2)
    diagonal = jax.random.uniform(diag_key, (term_total, PNO), jnp.float32, 0.7, 1.3)
    jitter = jnp.clip(jax.random.normal(jitter_key, (term_total, PNO, PNO), jnp.float32), -4.0, 4.0)
    identity = jnp.eye(PNO, dtype=jnp.float32)[None]
    return (identity * diagonal[:, :, None] + jitter * (0.6 / math.sqrt(PNO))).astype(jnp.bfloat16)


def draw_column_margin(key, part):
    return margin_draw(jax.random.fold_in(key, 11), TERMS)


def draw_row_margin(key, part):
    return margin_draw(jax.random.fold_in(key, 23), TERMS)


def send_lists(key, row_total):
    row_keys = jax.random.split(key, row_total)
    return jax.vmap(lambda row_key: jax.random.permutation(row_key, PAIRS_DEV)[:CAP])(row_keys).astype(jnp.int32)


def draw_column_sends(key, part):
    return send_lists(jax.random.fold_in(key, 31), N_OI * N_OJ * N_OI)


def draw_row_sends(key, part):
    return send_lists(jax.random.fold_in(key, 37), N_OI * N_OJ * N_OJ)


def draw_term_counts(key, part):
    devices_total = N_OI * N_OJ
    base_key, heavy_key, pick_key = jax.random.split(jax.random.fold_in(key, 41), 3)
    base = jax.random.randint(base_key, (devices_total, 2), max(1, TERMS_DEV // 8), TERMS_DEV // 3 + 1, dtype=jnp.int32)
    heavy = jax.random.randint(heavy_key, (devices_total, 2), 0, 8, dtype=jnp.int32) == 0
    chosen = jax.random.randint(pick_key, (1, 2), 0, devices_total, dtype=jnp.int32)
    filled = heavy | (jnp.arange(devices_total, dtype=jnp.int32)[:, None] == chosen)
    return jnp.where(filled, jnp.int32(TERMS_DEV), base).astype(jnp.int32)


def place_ends(values, key, smallest, largest):
    index_at = [jax.random.randint(jax.random.fold_in(key, axis), (), 0, length) for axis, length in enumerate(values.shape)]
    main_axis = values.shape.index(max(values.shape))
    neighbour = index_at[:main_axis] + [(index_at[main_axis] + 1) % values.shape[main_axis]] + index_at[main_axis + 1:]
    return values.at[tuple(index_at)].set(smallest).at[tuple(neighbour)].set(largest)


def shard_levels(key, dims, cuts, low, top_value):
    factor_of = 1.0
    for dim, parts in cuts:
        steps = jax.random.uniform(jax.random.fold_in(jax.random.fold_in(key, 6), dim), (parts,), jnp.float32, low / len(cuts), top_value / len(cuts))
        factor_of = factor_of * jnp.repeat(jnp.exp(steps), dims[dim] // parts).reshape((-1,) + (1,) * (len(dims) - 1 - dim))
    return factor_of


def noise(key, shape, scale, limit, shards=(), held_as=jnp.bfloat16):
    array = scale * jax.random.normal(key, shape, jnp.float32)
    if shards:
        array = array * shard_levels(key, shape, shards, -0.22, 0.18)
    return jnp.clip(array, -limit, limit).astype(held_as)


def setup_inputs(seed: int = 0) -> dict:
    splits = jax.random.split(jax.random.key(seed), 16)
    amplitudes = noise(splits[0], (PAIRS, PNO, PNO), 0.5, 4.0, ((0, 256),), jnp.float32)
    integrals = noise(splits[1], (PAIRS, PNO, PNO), 1.0, 6.0, ((0, 256),), jnp.float32)
    pno_energy = jnp.clip(jnp.exp(math.log(3.0) - 2.3025851 * jax.random.uniform(splits[2], (PAIRS, PNO), jnp.float32) ** shard_levels(splits[2], (PAIRS, PNO), ((0, 256),), -0.2, 0.2)), 0.3, 3.0)
    pair_shift = jnp.clip(0.5 + 1.5 * jax.random.uniform(splits[3], (PAIRS,), jnp.float32) ** shard_levels(splits[3], (PAIRS,), ((0, 256),), -0.2, 0.2), 0.5, 2.0)
    column_margin = draw_column_margin(jax.random.fold_in(splits[15], 71), 0)
    row_margin = draw_row_margin(jax.random.fold_in(splits[15], 71), 0)
    column_coupling = jnp.clip(jax.random.uniform(splits[6], (TERMS,), jnp.float32, -0.3, 0.3) * shard_levels(splits[6], (TERMS,), ((0, 256),), -0.4, 0.0), -0.3, 0.3)
    row_coupling = jnp.clip(jax.random.uniform(splits[7], (TERMS,), jnp.float32, -0.3, 0.3) * shard_levels(splits[7], (TERMS,), ((0, 256),), -0.4, 0.0), -0.3, 0.3)
    column_target = place_ends(jax.random.randint(splits[8], (TERMS,), 0, PAIRS_DEV), jax.random.fold_in(splits[8], 1), 0, PAIRS_DEV - 1).astype(jnp.int32)
    row_target = place_ends(jax.random.randint(splits[9], (TERMS,), 0, PAIRS_DEV), jax.random.fold_in(splits[9], 1), 0, PAIRS_DEV - 1).astype(jnp.int32)
    column_source = place_ends(jax.random.randint(splits[10], (TERMS,), 0, N_OI * CAP), jax.random.fold_in(splits[10], 1), 0, (N_OI * CAP) - 1).astype(jnp.int32)
    row_source = place_ends(jax.random.randint(splits[11], (TERMS,), 0, N_OJ * CAP), jax.random.fold_in(splits[11], 1), 0, (N_OJ * CAP) - 1).astype(jnp.int32)
    column_sends = draw_column_sends(jax.random.fold_in(splits[15], 71), 0)
    row_sends = draw_row_sends(jax.random.fold_in(splits[15], 71), 0)
    term_counts = draw_term_counts(jax.random.fold_in(splits[15], 71), 0)
    return {"amplitudes": amplitudes, "integrals": integrals, "pno_energy": pno_energy, "pair_shift": pair_shift, "column_margin": column_margin, "row_margin": row_margin, "column_coupling": column_coupling, "row_coupling": row_coupling, "column_target": column_target, "row_target": row_target, "column_source": column_source, "row_source": row_source, "column_sends": column_sends, "row_sends": row_sends, "term_counts": term_counts}


def term_sources(sources, sends, along_column):
    term_ids = jnp.arange(TERMS, dtype=jnp.int32)
    device = term_ids // TERMS_DEV
    first = device // N_OJ
    second = device % N_OJ
    source_peer = sources // CAP
    position = sources % CAP
    if along_column:
        sender = source_peer * N_OJ + second
        list_row = sender * N_OI + first
    else:
        sender = first * N_OJ + source_peer
        list_row = sender * N_OJ + second
    local_pair = sends[list_row.astype(jnp.int32), position.astype(jnp.int32)]
    return (sender * PAIRS_DEV + local_pair).astype(jnp.int32)


def term_weights(coupling, live_counts):
    term_ids = jnp.arange(TERMS, dtype=jnp.int32)
    device = term_ids // TERMS_DEV
    live_mask = (term_ids % TERMS_DEV) < live_counts[device]
    return jnp.where(live_mask, coupling, jnp.zeros_like(coupling))


def coupled(frozen, spare_allowance, source_pairs, weights, targets):
    def one_device(pieces):
        tile_slack_limit, block_sources, block_weights, block_targets = pieces
        tile_partitions = frozen[block_sources]
        central_split_index = jnp.einsum("ldq,lqp->ldp", tile_slack_limit.astype(jnp.float32), tile_partitions.astype(jnp.float32)).astype(jnp.bfloat16)
        congruent_projection = jnp.einsum("nlu,nyu->nly", central_split_index.astype(jnp.float32), tile_slack_limit.astype(jnp.float32))
        return jax.ops.segment_sum(congruent_projection * block_weights[:, None, None], block_targets, num_segments=PAIRS_DEV)

    devices_total = TERMS // TERMS_DEV
    result = lax.map(one_device, (spare_allowance.reshape(devices_total, TERMS_DEV, PNO, PNO),
                                  source_pairs.reshape(devices_total, TERMS_DEV),
                                  weights.reshape(devices_total, TERMS_DEV),
                                  targets.reshape(devices_total, TERMS_DEV)))
    return result.reshape(PAIRS, PNO, PNO)


def reference(amplitudes, integrals, pno_energy, pair_shift, column_margin, row_margin, column_coupling, row_coupling, column_target, row_target, column_source, row_source, column_sends, row_sends, term_counts):
    orbital_gap_divisor = pno_energy[:, :, None] + pno_energy[:, None, :] + pair_shift[:, None, None]
    column_pair = term_sources(column_source, column_sends, True)
    row_pair = term_sources(row_source, row_sends, False)
    column_weight = term_weights(column_coupling, term_counts[:, 0])
    row_weight = term_weights(row_coupling, term_counts[:, 1])
    residual = integrals
    for relaxation_round in range(ITERS):
        frozen = amplitudes.astype(jnp.bfloat16)
        column_coupled = coupled(frozen, column_margin, column_pair, column_weight, column_target)
        row_coupled = coupled(frozen, row_margin, row_pair, row_weight, row_target)
        residual = integrals + orbital_gap_divisor * amplitudes + column_coupled + row_coupled
        amplitudes = amplitudes - residual / orbital_gap_divisor
    return amplitudes, residual
```

```python
import functools

import jax
import jax.numpy as jnp
from jax import lax
from jax.experimental import pallas as pl
from jax.experimental.pallas import tpu as pltpu
from jax.sharding import PartitionSpec as P

ITERS = 2
CHUNK = 16
BOTH = ("oi", "oj")
VMEM = pl.BlockSpec(memory_space=pltpu.VMEM)
SMEM = pl.BlockSpec(memory_space=pltpu.SMEM)
ANY = pl.BlockSpec(memory_space=pl.ANY)
LIMIT = 32 * 1024 * 1024


def pack_pairs(frozen, column_sends, row_lists, column_out, row_outs):
    peers, capacity = column_sends.shape
    for peer in range(peers):
        for slot in range(capacity):
            column_out[peer * capacity + slot] = frozen[column_sends[peer, slot]]
    for step, out in enumerate(row_outs):
        for place in range(out.shape[0]):
            out[place] = frozen[row_lists[step * out.shape[0] + place]]


def first_pack(amplitudes, column_sends, row_lists, column_out, *rest):
    *row_outs, frozen = rest
    frozen[...] = amplitudes[...].astype(jnp.bfloat16)
    pack_pairs(frozen, column_sends, row_lists, column_out, row_outs)


def start_margins(margin, held, sems, live):
    for chunk in range(sems.shape[0]):
        rows = pl.ds(chunk * CHUNK, CHUNK)

        @pl.when(chunk * CHUNK < live)
        def _():
            pltpu.make_async_copy(margin.at[rows], held.at[rows], sems.at[chunk]).start()


def couple(margin, held, sems, live, blocks, source, target, coupling, total):
    def one_chunk(chunk, carry):
        rows = pl.ds(chunk * CHUNK, CHUNK)
        pltpu.make_async_copy(margin.at[rows], held.at[rows], sems.at[chunk]).wait()
        for step in range(CHUNK):
            term = chunk * CHUNK + step
            weight = jnp.where(term < live, coupling[term], 0.0)
            left = held[term]
            half = jnp.dot(left, blocks[source[term]], preferred_element_type=jnp.float32)
            whole = lax.dot_general(
                half.astype(jnp.bfloat16), left, (((1,), (1,)), ((), ())), preferred_element_type=jnp.float32
            )
            pair = target[term]
            total[pair] = total[pair] + weight * whole
        return carry

    lax.fori_loop(0, (live + CHUNK - 1) // CHUNK, one_chunk, 0)


def column_kernel(counts, source, target, coupling, blocks, margin, total, held, sems):
    live = counts[0, 0]
    start_margins(margin, held, sems, live)
    total[...] = jnp.zeros_like(total)
    couple(margin, held, sems, live, blocks, source, target, coupling, total)


def row_kernel(last, steps, counts, source, target, coupling, shift, column_sends, row_lists, energy, amplitudes, integrals,
               column_total, margin, swapped, *rest):
    pieces = rest[:steps]
    updated, residual = rest[steps : steps + 2]
    outs = rest[steps + 2 : -5]
    held, sems, blocks, total, frozen = rest[-5:]
    live = counts[0, 1]
    start_margins(margin, held, sems, live)
    total[...] = jnp.zeros_like(total)
    width = swapped.shape[1]
    for step in range(steps):
        blocks[step * 2 * width : step * 2 * width + width] = pieces[step][:width]
        blocks[step * 2 * width + width : (step + 1) * 2 * width] = swapped[step]
    couple(margin, held, sems, live, blocks, source, target, coupling, total)
    for pair in range(total.shape[0]):
        across = jnp.broadcast_to(energy[pair : pair + 1, :], total.shape[1:])
        gap = across.T + across + shift[pair]
        current = amplitudes[pair]
        left = integrals[pair] + gap * current + column_total[pair] + total[pair]
        fresh = current - left / gap
        updated[pair] = fresh
        residual[pair] = left
        if not last:
            frozen[pair] = fresh.astype(jnp.bfloat16)
    if not last:
        pack_pairs(frozen, column_sends, row_lists, outs[0], outs[1:])


def shards(
    amplitudes,
    integrals,
    pno_energy,
    pair_shift,
    column_margin,
    row_margin,
    column_coupling,
    row_coupling,
    column_target,
    row_target,
    column_source,
    row_source,
    column_sends,
    row_sends,
    term_counts,
):
    pairs, pno, _ = amplitudes.shape
    terms = column_margin.shape[0]
    peers, capacity = column_sends.shape
    steps = lax.axis_size("oj") // 2
    place = lax.axis_index("oj")
    chip, core = place // 2, place % 2

    up = (chip + jnp.arange(steps, dtype=jnp.int32)) % steps
    order = (up[:, None] * 2 + (core + jnp.arange(2, dtype=jnp.int32)[None, :]) % 2).reshape(-1)
    chosen = order[:, None] == jnp.arange(2 * steps, dtype=jnp.int32)[None, :]
    row_lists = jnp.sum(jnp.where(chosen[:, :, None], row_sends[None], 0), axis=1).reshape(-1)
    row_peer, row_slot = row_source // capacity, row_source % capacity
    down = (chip - row_peer // 2) % steps
    row_index = (down * 2 + (row_peer % 2 + core) % 2) * capacity + row_slot

    block = lambda count: jax.ShapeDtypeStruct((count, pno, pno), jnp.bfloat16)
    packed = (block(peers * capacity),) + (block(2 * capacity),) * steps
    whole = jax.ShapeDtypeStruct((pairs, pno, pno), jnp.float32)
    params = pltpu.CompilerParams(vmem_limit_bytes=LIMIT)
    margins = [
        pltpu.VMEM((terms, pno, pno), jnp.bfloat16),
        pltpu.SemaphoreType.DMA((terms // CHUNK,)),
    ]
    frozen = pltpu.VMEM((pairs, pno, pno), jnp.bfloat16)
    cost = pl.CostEstimate(flops=4 * terms * pno**3, bytes_accessed=2 * terms * pno**2, transcendentals=0)

    outs = pl.pallas_call(
        first_pack,
        out_shape=packed,
        in_specs=[VMEM, SMEM, SMEM],
        out_specs=(VMEM,) * (steps + 1),
        scratch_shapes=[frozen],
        compiler_params=params,
        name="pack",
    )(amplitudes, column_sends, row_lists)
    residual = integrals
    for sweep in range(ITERS):
        last = sweep == ITERS - 1
        pieces = [outs[1]]
        for step in range(1, steps):
            ring = [(c + 2 * z, c + 2 * ((z + step) % steps)) for z in range(steps) for c in range(2)]
            pieces.append(lax.ppermute(outs[1 + step], "oj", ring))
        column_blocks = lax.all_to_all(outs[0], "oi", split_axis=0, concat_axis=0, tiled=True)
        other = jnp.stack([piece[capacity:] for piece in pieces])
        swapped = lax.ppermute(other, "oj", [(i, i ^ 1) for i in range(2 * steps)])
        column_total = pl.pallas_call(
            column_kernel,
            out_shape=whole,
            in_specs=[SMEM] * 4 + [VMEM, ANY],
            out_specs=VMEM,
            scratch_shapes=margins,
            compiler_params=params,
            cost_estimate=cost,
            name="column_terms",
        )(term_counts, column_source, column_target, column_coupling, column_blocks, column_margin)
        results = pl.pallas_call(
            functools.partial(row_kernel, last, steps),
            out_shape=(whole, whole) + (() if last else packed),
            in_specs=[SMEM] * 7 + [VMEM] * 4 + [ANY] + [VMEM] * (1 + steps),
            out_specs=(VMEM,) * (2 if last else 3 + steps),
            scratch_shapes=margins
            + [pltpu.VMEM((2 * steps * capacity, pno, pno), jnp.bfloat16), pltpu.VMEM((pairs, pno, pno), jnp.float32), frozen],
            compiler_params=params,
            cost_estimate=cost,
            name="row_terms",
        )(term_counts, row_index, row_target, row_coupling, pair_shift, column_sends, row_lists, pno_energy, amplitudes,
          integrals, column_total, row_margin, swapped, *pieces)
        amplitudes, residual, *outs = results
    return (amplitudes, residual)


def solution(mesh):
    in_specs = (
        P(BOTH, None, None),
        P(BOTH, None, None),
        P(BOTH, None),
        P(BOTH),
        P(BOTH, None, None),
        P(BOTH, None, None),
        P(BOTH),
        P(BOTH),
        P(BOTH),
        P(BOTH),
        P(BOTH),
        P(BOTH),
        P(BOTH, None),
        P(BOTH, None),
        P(BOTH, None),
    )
    out_specs = (P(BOTH, None, None), P(BOTH, None, None))
    return jax.shard_map(shards, mesh=mesh, in_specs=in_specs, out_specs=out_specs, check_vma=False)
```

```python
import functools

import jax
import jax.numpy as jnp
from jax import lax
from jax.experimental import pallas as pl
from jax.experimental.pallas import tpu as pltpu
from jax.sharding import PartitionSpec as P

ITERS = 2
CHUNK = 32
BOTH = ("oi", "oj")
VMEM = pl.BlockSpec(memory_space=pltpu.VMEM)
SMEM = pl.BlockSpec(memory_space=pltpu.SMEM)
ANY = pl.BlockSpec(memory_space=pl.ANY)
HBM = pl.BlockSpec(memory_space=pltpu.HBM)
LIMIT = 32 * 1024 * 1024


def pack_pairs(frozen, column_sends, row_sends, column_out, row_out):
    peers, capacity = column_sends.shape
    pairs, pno, _ = frozen.shape
    for pair in range(pairs):
        row_out[pair * pno : (pair + 1) * pno, :] = frozen[pair]
    row_out[pairs * pno :, :] = jnp.zeros((row_out.shape[0] - pairs * pno, pno), row_out.dtype)
    row_out[pairs * pno :, :capacity] = row_sends[...].astype(jnp.float32).astype(row_out.dtype)
    for peer in range(peers):
        for slot in range(capacity):
            column_out[peer * capacity + slot] = frozen[column_sends[peer, slot]]


def first_pack(amplitudes, column_sends, row_sends, column_out, row_out, frozen):
    frozen[...] = amplitudes[...].astype(jnp.bfloat16)
    pack_pairs(frozen, column_sends, row_sends, column_out, row_out)


def start_margins(margin, held, sems, live):
    for chunk in range(sems.shape[0]):
        rows = pl.ds(chunk * CHUNK, CHUNK)

        @pl.when(chunk * CHUNK < live)
        def _():
            pltpu.make_async_copy(margin.at[rows], held.at[rows], sems.at[chunk]).start()


def couple(margin, held, sems, live, block, target, coupling, total):
    def one_chunk(chunk, carry):
        rows = pl.ds(chunk * CHUNK, CHUNK)
        pltpu.make_async_copy(margin.at[rows], held.at[rows], sems.at[chunk]).wait()
        terms = [chunk * CHUNK + step for step in range(CHUNK)]
        halves = [
            jnp.dot(held[term], block(term), preferred_element_type=jnp.float32).astype(jnp.bfloat16) for term in terms
        ]
        wholes = [
            lax.dot_general(half, held[term], (((1,), (1,)), ((), ())), preferred_element_type=jnp.float32)
            for half, term in zip(halves, terms)
        ]
        for whole, term in zip(wholes, terms):
            weight = jnp.where(term < live, coupling(term), 0.0)
            pair = target(term)
            total[pair] = total[pair] + weight * whole
        return carry

    lax.fori_loop(0, (live + CHUNK - 1) // CHUNK, one_chunk, 0)


def column_kernel(whole_numbers, reals, blocks, margin, total, held, sems):
    live = whole_numbers[4, 0]
    start_margins(margin, held, sems, live)
    total[...] = jnp.zeros_like(total)
    couple(
        margin, held, sems, live, lambda term: blocks[whole_numbers[0, term]], lambda term: whole_numbers[1, term],
        lambda term: reals[0, term], total,
    )


def row_kernel(last, width, whole_numbers, reals, column_sends, row_sends, energy, amplitudes, integrals, column_total, margin,
               *rest):
    pieces, rest = rest[:11], rest[11:]
    updated, residual = rest[:2]
    held, sems, blocks, stage, listed, piece_sems, list_sem, total, frozen = rest[-9:]
    live = whole_numbers[4, 1]
    pno = energy.shape[1]
    half = pieces[7].shape[0]
    plan = [(0, 0, width, 0, 0), (1, 0, width, 7, 0), (2, 0, width, 1, 0), (3, 0, width, 6, 0), (4, 0, width, 2, 0),
            (5, 0, width, 5, 0), (6, 0, width, 3, 0), (7, 0, half, 4, 0), (8, 0, width - half, 4, half)]
    plan += [(9, i * width, width, 8 + place, 0) for i, place in enumerate((0, 7, 1, 6, 2))]
    plan += [(10, i * width, width, 8 + place, 0) for i, place in enumerate((5, 3, 4))]
    copies = [
        pltpu.make_async_copy(pieces[piece].at[pl.ds(row, rows)], blocks.at[pl.ds(place * width + there, rows)], piece_sems.at[i])
        for i, (piece, row, rows, place, there) in enumerate(plan)
    ]
    for copy in copies:
        copy.start()
    start_margins(margin, held, sems, live)
    total[...] = jnp.zeros_like(total)
    for copy in copies:
        copy.wait()
    me = whole_numbers[4, 2]
    spare = stage.shape[0]
    for place in range(16):
        lists = blocks[place * width + width - 16 : (place + 1) * width, :].astype(jnp.float32)
        mine = lax.broadcasted_iota(jnp.int32, lists.shape, 0) == me
        stage[place : place + 1, :] = jnp.sum(jnp.where(mine, lists, 0.0), axis=0, keepdims=True).astype(jnp.int32)
    to_scalars = pltpu.make_async_copy(stage, listed, list_sem)
    to_scalars.start()
    to_scalars.wait()

    def block(term):
        place, slot = whole_numbers[2, term] // 2, whole_numbers[2, term] % 2
        row = place * width + listed[place, slot] * pno
        return blocks[pl.ds(pl.multiple_of(row, 16), pno), :]

    couple(margin, held, sems, live, block, lambda term: whole_numbers[3, term], lambda term: reals[1, term], total)
    for pair in range(total.shape[0]):
        across = jnp.broadcast_to(energy[pair : pair + 1, :], total.shape[1:])
        gap = across.T + across + reals[2, pair]
        current = amplitudes[pair]
        left = integrals[pair] + gap * current + column_total[pair] + total[pair]
        fresh = current - left / gap
        updated[pair] = fresh
        residual[pair] = left
        if not last:
            frozen[pair] = fresh.astype(jnp.bfloat16)
    if not last:
        pack_pairs(frozen, column_sends, row_sends, rest[2], rest[3])


def along_z(piece, step):
    chips = lax.axis_size("oj") // 2
    return lax.ppermute(piece, "oj", [(c + 2 * z, c + 2 * ((z + step) % chips)) for z in range(chips) for c in range(2)])


def swap_cores(piece):
    return lax.ppermute(piece, "oj", [(i, i ^ 1) for i in range(lax.axis_size("oj"))])


def gather_rows(own, half):
    up1, down1, up2, down2 = (along_z(own, step) for step in (1, -1, 2, -2))
    near = jnp.concatenate([own, up1, down1, up2, down2])
    up3, down3 = along_z(up2, 1), along_z(down2, -1)
    up4, down4 = along_z(up2[:half], 2), along_z(down2[half:], -2)
    far = jnp.concatenate([up3, down3, up4, down4])
    return [own, up1, down1, up2, down2, up3, down3, up4, down4, swap_cores(near), swap_cores(far)]


def shards(
    amplitudes,
    integrals,
    pno_energy,
    pair_shift,
    column_margin,
    row_margin,
    column_coupling,
    row_coupling,
    column_target,
    row_target,
    column_source,
    row_source,
    column_sends,
    row_sends,
    term_counts,
):
    pairs, pno, _ = amplitudes.shape
    terms = column_margin.shape[0]
    peers, capacity = column_sends.shape
    chips = lax.axis_size("oj") // 2
    me = lax.axis_index("oj")
    chip, core = me // 2, me % 2

    row_peer, row_slot = row_source // capacity, row_source % capacity
    place = (row_peer // 2 - chip) % chips + chips * ((row_peer + core) % 2)
    facts = jnp.concatenate([term_counts[0], me[None].astype(jnp.int32), jnp.zeros((terms - 3,), jnp.int32)])
    whole_numbers = jnp.stack([column_source, column_target, place * 2 + row_slot, row_target, facts])
    reals = jnp.stack([column_coupling, row_coupling, jnp.pad(pair_shift, (0, terms - pairs))])

    width = pairs * pno + 16
    packed = (
        jax.ShapeDtypeStruct((peers * capacity, pno, pno), jnp.bfloat16),
        jax.ShapeDtypeStruct((width, pno), jnp.bfloat16),
    )
    whole = jax.ShapeDtypeStruct((pairs, pno, pno), jnp.float32)
    params = pltpu.CompilerParams(vmem_limit_bytes=LIMIT)
    margins = [
        pltpu.VMEM((terms, pno, pno), jnp.bfloat16),
        pltpu.SemaphoreType.DMA((terms // CHUNK,)),
    ]
    frozen = pltpu.VMEM((pairs, pno, pno), jnp.bfloat16)
    cost = pl.CostEstimate(flops=4 * terms * pno**3, bytes_accessed=2 * terms * pno**2, transcendentals=0)

    column_out, row_out = pl.pallas_call(
        first_pack,
        out_shape=packed,
        in_specs=[VMEM, SMEM, VMEM],
        out_specs=(VMEM, VMEM),
        scratch_shapes=[frozen],
        compiler_params=params,
        name="pack",
    )(amplitudes, column_sends, row_sends)
    residual = integrals
    for sweep in range(ITERS):
        last = sweep == ITERS - 1
        column_blocks = lax.all_to_all(column_out, "oi", split_axis=0, concat_axis=0, tiled=True)
        pieces = gather_rows(row_out, pairs // 2 * pno)
        column_total = pl.pallas_call(
            column_kernel,
            out_shape=whole,
            in_specs=[SMEM, SMEM, VMEM, HBM],
            out_specs=VMEM,
            scratch_shapes=margins,
            compiler_params=params,
            cost_estimate=cost,
            name="column_terms",
        )(whole_numbers, reals, column_blocks, column_margin)
        amplitudes, residual, *outs = pl.pallas_call(
            functools.partial(row_kernel, last, width),
            out_shape=(whole, whole) + (() if last else packed),
            in_specs=[SMEM] * 3 + [VMEM] * 5 + [HBM] + [ANY] * len(pieces),
            out_specs=(VMEM,) * (2 if last else 4),
            scratch_shapes=margins
            + [
                pltpu.VMEM((2 * chips * width, pno), jnp.bfloat16),
                pltpu.VMEM((2 * chips, pno), jnp.int32),
                pltpu.SMEM((2 * chips, pno), jnp.int32),
                pltpu.SemaphoreType.DMA((17,)),
                pltpu.SemaphoreType.DMA,
                pltpu.VMEM((pairs, pno, pno), jnp.float32),
                frozen,
            ],
            compiler_params=params,
            cost_estimate=cost,
            name="row_terms",
        )(whole_numbers, reals, column_sends, row_sends, pno_energy, amplitudes, integrals, column_total, row_margin, *pieces)
        if not last:
            column_out, row_out = outs
    return (amplitudes, residual)


def solution(mesh):
    in_specs = (
        P(BOTH, None, None),
        P(BOTH, None, None),
        P(BOTH, None),
        P(BOTH),
        P(BOTH, None, None),
        P(BOTH, None, None),
        P(BOTH),
        P(BOTH),
        P(BOTH),
        P(BOTH),
        P(BOTH),
        P(BOTH),
        P(BOTH, None),
        P(BOTH, None),
        P(BOTH, None),
    )
    out_specs = (P(BOTH, None, None), P(BOTH, None, None))
    return jax.shard_map(shards, mesh=mesh, in_specs=in_specs, out_specs=out_specs, check_vma=False)
```

```python
import functools

import jax
import jax.numpy as jnp
from jax import lax
from jax.experimental import pallas as pl
from jax.experimental.pallas import tpu as pltpu
from jax.sharding import PartitionSpec as P

ITERS = 2
CHUNK = 32
BOTH = ("oi", "oj")
VMEM = pl.BlockSpec(memory_space=pltpu.VMEM)
SMEM = pl.BlockSpec(memory_space=pltpu.SMEM)
ANY = pl.BlockSpec(memory_space=pl.ANY)
HBM = pl.BlockSpec(memory_space=pltpu.HBM)
LIMIT = 50 * 1024 * 1024


def pack_pairs(frozen, column_sends, row_sends, column_out, row_out):
    peers, capacity = column_sends.shape
    pairs, pno, _ = frozen.shape
    for pair in range(pairs):
        row_out[pair * pno : (pair + 1) * pno, :] = frozen[pair]
    row_out[pairs * pno :, :] = jnp.zeros((row_out.shape[0] - pairs * pno, pno), row_out.dtype)
    row_out[pairs * pno :, :capacity] = row_sends[...].astype(jnp.float32).astype(row_out.dtype)
    for peer in range(peers):
        for slot in range(capacity):
            column_out[peer * capacity + slot] = frozen[column_sends[peer, slot]]


def first_pack(amplitudes, column_sends, row_sends, column_out, row_out, frozen):
    frozen[...] = amplitudes[...].astype(jnp.bfloat16)
    pack_pairs(frozen, column_sends, row_sends, column_out, row_out)


def start_margins(margin, held, sems, live):
    for chunk in range(sems.shape[0]):
        rows = pl.ds(chunk * CHUNK, CHUNK)

        @pl.when(chunk * CHUNK < live)
        def _():
            pltpu.make_async_copy(margin.at[rows], held.at[rows], sems.at[chunk]).start()


def couple(margin, held, sems, live, block, target, coupling, total):
    def one_chunk(chunk, carry):
        rows = pl.ds(chunk * CHUNK, CHUNK)
        pltpu.make_async_copy(margin.at[rows], held.at[rows], sems.at[chunk]).wait()
        terms = [chunk * CHUNK + step for step in range(CHUNK)]
        halves = [
            jnp.dot(held[term], block(term), preferred_element_type=jnp.float32).astype(jnp.bfloat16) for term in terms
        ]
        wholes = [
            lax.dot_general(half, held[term], (((1,), (1,)), ((), ())), preferred_element_type=jnp.float32)
            for half, term in zip(halves, terms)
        ]
        for whole, term in zip(wholes, terms):
            weight = jnp.where(term < live, coupling(term), 0.0)
            pair = target(term)
            total[pair] = total[pair] + weight * whole
        return carry

    lax.fori_loop(0, (live + CHUNK - 1) // CHUNK, one_chunk, 0)


def row_kernel(width, whole_numbers, reals, margin, *rest):
    pieces, rest = rest[:11], rest[11:]
    total, held, sems, blocks, stage, listed, piece_sems, list_sem = rest
    live = whole_numbers[4, 1]
    pno = held.shape[-1]
    half = pieces[7].shape[0]
    plan = [(0, 0, width, 0, 0), (1, 0, width, 7, 0), (2, 0, width, 1, 0), (3, 0, width, 6, 0), (4, 0, width, 2, 0),
            (5, 0, width, 5, 0), (6, 0, width, 3, 0), (7, 0, half, 4, 0), (8, 0, width - half, 4, half)]
    plan += [(9, i * width, width, 8 + place, 0) for i, place in enumerate((0, 7, 1, 6, 2))]
    plan += [(10, i * width, width, 8 + place, 0) for i, place in enumerate((5, 3, 4))]
    copies = [
        pltpu.make_async_copy(pieces[piece].at[pl.ds(row, rows)], blocks.at[pl.ds(place * width + there, rows)], piece_sems.at[i])
        for i, (piece, row, rows, place, there) in enumerate(plan)
    ]
    for copy in copies:
        copy.start()
    start_margins(margin, held, sems, live)
    total[...] = jnp.zeros_like(total)
    for copy in copies:
        copy.wait()
    me = whole_numbers[4, 2]
    for place in range(stage.shape[0]):
        lists = blocks[place * width + width - 16 : (place + 1) * width, :].astype(jnp.float32)
        mine = lax.broadcasted_iota(jnp.int32, lists.shape, 0) == me
        stage[place : place + 1, :] = jnp.sum(jnp.where(mine, lists, 0.0), axis=0, keepdims=True).astype(jnp.int32)
    to_scalars = pltpu.make_async_copy(stage, listed, list_sem)
    to_scalars.start()
    to_scalars.wait()

    def block(term):
        place, slot = whole_numbers[2, term] // 2, whole_numbers[2, term] % 2
        row = place * width + listed[place, slot] * pno
        return blocks[pl.ds(pl.multiple_of(row, 16), pno), :]

    couple(margin, held, sems, live, block, lambda term: whole_numbers[3, term], lambda term: reals[1, term], total)


def column_kernel(last, whole_numbers, reals, column_sends, row_sends, energy, amplitudes, integrals, row_total, blocks, margin,
                  *rest):
    updated, residual = rest[:2]
    held, sems, total, frozen = rest[-4:]
    live = whole_numbers[4, 0]
    start_margins(margin, held, sems, live)
    total[...] = jnp.zeros_like(total)
    couple(
        margin, held, sems, live, lambda term: blocks[whole_numbers[0, term]], lambda term: whole_numbers[1, term],
        lambda term: reals[0, term], total,
    )
    for pair in range(total.shape[0]):
        across = jnp.broadcast_to(energy[pair : pair + 1, :], total.shape[1:])
        gap = across.T + across + reals[2, pair]
        current = amplitudes[pair]
        left = integrals[pair] + gap * current + total[pair] + row_total[pair]
        fresh = current - left / gap
        updated[pair] = fresh
        residual[pair] = left
        if not last:
            frozen[pair] = fresh.astype(jnp.bfloat16)
    if not last:
        pack_pairs(frozen, column_sends, row_sends, rest[2], rest[3])


def along_z(piece, step):
    chips = lax.axis_size("oj") // 2
    return lax.ppermute(piece, "oj", [(c + 2 * z, c + 2 * ((z + step) % chips)) for z in range(chips) for c in range(2)])


def swap_cores(piece):
    return lax.ppermute(piece, "oj", [(i, i ^ 1) for i in range(lax.axis_size("oj"))])


def gather_rows(own, half):
    up1, down1, up2, down2 = (along_z(own, step) for step in (1, -1, 2, -2))
    near = jnp.concatenate([own, up1, down1, up2, down2])
    up3, down3 = along_z(up2, 1), along_z(down2, -1)
    up4, down4 = along_z(up2[:half], 2), along_z(down2[half:], -2)
    far = jnp.concatenate([up3, down3, up4, down4])
    return [own, up1, down1, up2, down2, up3, down3, up4, down4, swap_cores(near), swap_cores(far)]


def shards(
    amplitudes,
    integrals,
    pno_energy,
    pair_shift,
    column_margin,
    row_margin,
    column_coupling,
    row_coupling,
    column_target,
    row_target,
    column_source,
    row_source,
    column_sends,
    row_sends,
    term_counts,
):
    pairs, pno, _ = amplitudes.shape
    terms = column_margin.shape[0]
    peers, capacity = column_sends.shape
    chips = lax.axis_size("oj") // 2
    me = lax.axis_index("oj")
    chip, core = me // 2, me % 2

    row_peer, row_slot = row_source // capacity, row_source % capacity
    place = (row_peer // 2 - chip) % chips + chips * ((row_peer + core) % 2)
    facts = jnp.concatenate([term_counts[0], me[None].astype(jnp.int32), jnp.zeros((terms - 3,), jnp.int32)])
    whole_numbers = jnp.stack([column_source, column_target, place * 2 + row_slot, row_target, facts])
    reals = jnp.stack([column_coupling, row_coupling, jnp.pad(pair_shift, (0, terms - pairs))])

    width = pairs * pno + 16
    packed = (
        jax.ShapeDtypeStruct((peers * capacity, pno, pno), jnp.bfloat16),
        jax.ShapeDtypeStruct((width, pno), jnp.bfloat16),
    )
    whole = jax.ShapeDtypeStruct((pairs, pno, pno), jnp.float32)
    params = pltpu.CompilerParams(vmem_limit_bytes=LIMIT)
    margins = [
        pltpu.VMEM((terms, pno, pno), jnp.bfloat16),
        pltpu.SemaphoreType.DMA((terms // CHUNK,)),
    ]
    frozen = pltpu.VMEM((pairs, pno, pno), jnp.bfloat16)
    cost = pl.CostEstimate(flops=4 * terms * pno**3, bytes_accessed=2 * terms * pno**2, transcendentals=0)

    column_out, row_out = pl.pallas_call(
        first_pack,
        out_shape=packed,
        in_specs=[VMEM, SMEM, VMEM],
        out_specs=(VMEM, VMEM),
        scratch_shapes=[frozen],
        compiler_params=params,
        name="pack",
    )(amplitudes, column_sends, row_sends)
    residual = integrals
    for sweep in range(ITERS):
        last = sweep == ITERS - 1
        column_blocks = lax.all_to_all(column_out, "oi", split_axis=0, concat_axis=0, tiled=True)
        pieces = gather_rows(row_out, pairs // 2 * pno)
        row_total = pl.pallas_call(
            functools.partial(row_kernel, width),
            out_shape=whole,
            in_specs=[SMEM] * 2 + [HBM] + [ANY] * len(pieces),
            out_specs=VMEM,
            scratch_shapes=margins
            + [
                pltpu.VMEM((2 * chips * width, pno), jnp.bfloat16),
                pltpu.VMEM((2 * chips, pno), jnp.int32),
                pltpu.SMEM((2 * chips, pno), jnp.int32),
                pltpu.SemaphoreType.DMA((17,)),
                pltpu.SemaphoreType.DMA,
            ],
            compiler_params=params,
            cost_estimate=cost,
            name="row_terms",
        )(whole_numbers, reals, row_margin, *pieces)
        amplitudes, residual, *outs = pl.pallas_call(
            functools.partial(column_kernel, last),
            out_shape=(whole, whole) + (() if last else packed),
            in_specs=[SMEM] * 3 + [VMEM] * 6 + [HBM],
            out_specs=(VMEM,) * (2 if last else 4),
            scratch_shapes=margins + [pltpu.VMEM((pairs, pno, pno), jnp.float32), frozen],
            compiler_params=params,
            cost_estimate=cost,
            name="column_terms",
        )(whole_numbers, reals, column_sends, row_sends, pno_energy, amplitudes, integrals, row_total, column_blocks,
          column_margin)
        if not last:
            column_out, row_out = outs
    return (amplitudes, residual)


def solution(mesh):
    in_specs = (
        P(BOTH, None, None),
        P(BOTH, None, None),
        P(BOTH, None),
        P(BOTH),
        P(BOTH, None, None),
        P(BOTH, None, None),
        P(BOTH),
        P(BOTH),
        P(BOTH),
        P(BOTH),
        P(BOTH),
        P(BOTH),
        P(BOTH, None),
        P(BOTH, None),
        P(BOTH, None),
    )
    out_specs = (P(BOTH, None, None), P(BOTH, None, None))
    return jax.shard_map(shards, mesh=mesh, in_specs=in_specs, out_specs=out_specs, check_vma=False)
```

```python
import functools

import jax
import jax.numpy as jnp
from jax import lax
from jax.experimental import pallas as pl
from jax.experimental.pallas import tpu as pltpu
from jax.sharding import PartitionSpec as P

ITERS = 2
CHUNK = 32
BOTH = ("oi", "oj")
VMEM = pl.BlockSpec(memory_space=pltpu.VMEM)
SMEM = pl.BlockSpec(memory_space=pltpu.SMEM)
ANY = pl.BlockSpec(memory_space=pl.ANY)
HBM = pl.BlockSpec(memory_space=pltpu.HBM)
LIMIT = 50 * 1024 * 1024


def pack_pairs(frozen, column_sends, row_sends, column_out, row_out):
    peers, capacity = column_sends.shape
    pairs, pno, _ = frozen.shape
    for pair in range(pairs):
        row_out[pair * pno : (pair + 1) * pno, :] = frozen[pair]
    row_out[pairs * pno :, :] = jnp.zeros((row_out.shape[0] - pairs * pno, pno), row_out.dtype)
    row_out[pairs * pno :, :capacity] = row_sends[...].astype(jnp.float32).astype(row_out.dtype)
    for peer in range(peers):
        for slot in range(capacity):
            column_out[peer * capacity + slot] = frozen[column_sends[peer, slot]]


def first_pack(amplitudes, column_sends, row_sends, column_out, row_out, frozen):
    frozen[...] = amplitudes[...].astype(jnp.bfloat16)
    pack_pairs(frozen, column_sends, row_sends, column_out, row_out)


def start_margins(margin, held, sems, live):
    for chunk in range(sems.shape[0]):
        rows = pl.ds(chunk * CHUNK, CHUNK)

        @pl.when(chunk * CHUNK < live)
        def _():
            pltpu.make_async_copy(margin.at[rows], held.at[rows], sems.at[chunk]).start()


def couple(margin, held, sems, live, block, target, coupling, total):
    def one_chunk(chunk, carry):
        rows = pl.ds(chunk * CHUNK, CHUNK)
        pltpu.make_async_copy(margin.at[rows], held.at[rows], sems.at[chunk]).wait()
        terms = [chunk * CHUNK + step for step in range(CHUNK)]
        halves = [
            jnp.dot(held[term], block(term), preferred_element_type=jnp.float32).astype(jnp.bfloat16) for term in terms
        ]
        wholes = [
            lax.dot_general(half, held[term], (((1,), (1,)), ((), ())), preferred_element_type=jnp.float32)
            for half, term in zip(halves, terms)
        ]
        for whole, term in zip(wholes, terms):
            weight = jnp.where(term < live, coupling(term), 0.0)
            pair = target(term)
            total[pair] = total[pair] + weight * whole
        return carry

    lax.fori_loop(0, (live + CHUNK - 1) // CHUNK, one_chunk, 0)


def sweep_kernel(last, width, whole_numbers, reals, column_sends, row_sends, energy, amplitudes, integrals, column_blocks,
                 column_margin, row_margin, *rest):
    pieces, rest = rest[:11], rest[11:]
    updated, residual = rest[:2]
    (column_held, row_held, column_sems, row_sems, blocks, stage, listed, piece_sems, list_sem, column_total, row_total,
     frozen) = rest[-12:]
    column_live, row_live, me = whole_numbers[4, 0], whole_numbers[4, 1], whole_numbers[4, 2]
    pno = energy.shape[1]
    half = pieces[7].shape[0]
    plan = [(0, 0, width, 0, 0), (1, 0, width, 7, 0), (2, 0, width, 1, 0), (3, 0, width, 6, 0), (4, 0, width, 2, 0),
            (5, 0, width, 5, 0), (6, 0, width, 3, 0), (7, 0, half, 4, 0), (8, 0, width - half, 4, half)]
    plan += [(9, i * width, width, 8 + place, 0) for i, place in enumerate((0, 7, 1, 6, 2))]
    plan += [(10, i * width, width, 8 + place, 0) for i, place in enumerate((5, 3, 4))]
    copies = [
        pltpu.make_async_copy(pieces[piece].at[pl.ds(row, rows)], blocks.at[pl.ds(place * width + there, rows)], piece_sems.at[i])
        for i, (piece, row, rows, place, there) in enumerate(plan)
    ]
    for copy in copies:
        copy.start()
    start_margins(column_margin, column_held, column_sems, column_live)
    start_margins(row_margin, row_held, row_sems, row_live)
    column_total[...] = jnp.zeros_like(column_total)
    row_total[...] = jnp.zeros_like(row_total)
    for copy in copies:
        copy.wait()
    for place in range(stage.shape[0]):
        lists = blocks[place * width + width - 16 : (place + 1) * width, :].astype(jnp.float32)
        mine = lax.broadcasted_iota(jnp.int32, lists.shape, 0) == me
        stage[place : place + 1, :] = jnp.sum(jnp.where(mine, lists, 0.0), axis=0, keepdims=True).astype(jnp.int32)
    to_scalars = pltpu.make_async_copy(stage, listed, list_sem)
    to_scalars.start()
    couple(
        column_margin, column_held, column_sems, column_live, lambda term: column_blocks[whole_numbers[0, term]],
        lambda term: whole_numbers[1, term], lambda term: reals[0, term], column_total,
    )
    to_scalars.wait()

    def block(term):
        place, slot = whole_numbers[2, term] // 2, whole_numbers[2, term] % 2
        row = place * width + listed[place, slot] * pno
        return blocks[pl.ds(pl.multiple_of(row, 16), pno), :]

    couple(
        row_margin, row_held, row_sems, row_live, block, lambda term: whole_numbers[3, term], lambda term: reals[1, term],
        row_total,
    )
    for pair in range(row_total.shape[0]):
        across = jnp.broadcast_to(energy[pair : pair + 1, :], row_total.shape[1:])
        gap = across.T + across + reals[2, pair]
        current = amplitudes[pair]
        left = integrals[pair] + gap * current + column_total[pair] + row_total[pair]
        fresh = current - left / gap
        updated[pair] = fresh
        residual[pair] = left
        if not last:
            frozen[pair] = fresh.astype(jnp.bfloat16)
    if not last:
        pack_pairs(frozen, column_sends, row_sends, rest[2], rest[3])


def along_z(piece, step):
    chips = lax.axis_size("oj") // 2
    return lax.ppermute(piece, "oj", [(c + 2 * z, c + 2 * ((z + step) % chips)) for z in range(chips) for c in range(2)])


def swap_cores(piece):
    return lax.ppermute(piece, "oj", [(i, i ^ 1) for i in range(lax.axis_size("oj"))])


def gather_rows(own, half, numbers):
    up1, down1, up2, down2 = (along_z(own, step) for step in (1, -1, 2, -2))
    near = jnp.concatenate([own, up1, down1, up2, down2])
    up3, down3 = along_z(up2, 1), along_z(down2, -1)
    up4, down4 = along_z(up2[:half], 2), along_z(down2[half:], -2)
    up3, down3, up4, down4, numbers = lax.optimization_barrier((up3, down3, up4, down4, numbers))
    far = jnp.concatenate([up3, down3, up4, down4])
    return [own, up1, down1, up2, down2, up3, down3, up4, down4, swap_cores(near), swap_cores(far)], numbers


def shards(
    amplitudes,
    integrals,
    pno_energy,
    pair_shift,
    column_margin,
    row_margin,
    column_coupling,
    row_coupling,
    column_target,
    row_target,
    column_source,
    row_source,
    column_sends,
    row_sends,
    term_counts,
):
    pairs, pno, _ = amplitudes.shape
    terms = column_margin.shape[0]
    peers, capacity = column_sends.shape
    chips = lax.axis_size("oj") // 2
    me = lax.axis_index("oj")
    chip, core = me // 2, me % 2

    row_peer, row_slot = row_source // capacity, row_source % capacity
    place = (row_peer // 2 - chip) % chips + chips * ((row_peer + core) % 2)
    facts = jnp.concatenate([term_counts[0], me[None].astype(jnp.int32), jnp.zeros((terms - 3,), jnp.int32)])
    whole_numbers = jnp.stack([column_source, column_target, place * 2 + row_slot, row_target, facts])
    reals = jnp.stack([column_coupling, row_coupling, jnp.pad(pair_shift, (0, terms - pairs))])

    width = pairs * pno + 16
    packed = (
        jax.ShapeDtypeStruct((peers * capacity, pno, pno), jnp.bfloat16),
        jax.ShapeDtypeStruct((width, pno), jnp.bfloat16),
    )
    whole = jax.ShapeDtypeStruct((pairs, pno, pno), jnp.float32)
    params = pltpu.CompilerParams(vmem_limit_bytes=LIMIT)
    margins = [pltpu.VMEM((terms, pno, pno), jnp.bfloat16)] * 2 + [pltpu.SemaphoreType.DMA((terms // CHUNK,))] * 2
    frozen = pltpu.VMEM((pairs, pno, pno), jnp.bfloat16)
    cost = pl.CostEstimate(flops=8 * terms * pno**3, bytes_accessed=4 * terms * pno**2, transcendentals=0)

    column_out, row_out = pl.pallas_call(
        first_pack,
        out_shape=packed,
        in_specs=[VMEM, SMEM, VMEM],
        out_specs=(VMEM, VMEM),
        scratch_shapes=[frozen],
        compiler_params=params,
        name="pack",
    )(amplitudes, column_sends, row_sends)
    residual = integrals
    for sweep in range(ITERS):
        last = sweep == ITERS - 1
        column_blocks = lax.all_to_all(column_out, "oi", split_axis=0, concat_axis=0, tiled=True)
        pieces, (whole_numbers, reals) = gather_rows(row_out, pairs // 2 * pno, (whole_numbers, reals))
        amplitudes, residual, *outs = pl.pallas_call(
            functools.partial(sweep_kernel, last, width),
            out_shape=(whole, whole) + (() if last else packed),
            in_specs=[SMEM] * 3 + [VMEM] * 5 + [HBM] * 2 + [ANY] * len(pieces),
            out_specs=(VMEM,) * (2 if last else 4),
            scratch_shapes=margins
            + [
                pltpu.VMEM((2 * chips * width, pno), jnp.bfloat16),
                pltpu.VMEM((2 * chips, pno), jnp.int32),
                pltpu.SMEM((2 * chips, pno), jnp.int32),
                pltpu.SemaphoreType.DMA((17,)),
                pltpu.SemaphoreType.DMA,
                pltpu.VMEM((pairs, pno, pno), jnp.float32),
                pltpu.VMEM((pairs, pno, pno), jnp.float32),
                frozen,
            ],
            compiler_params=params,
            cost_estimate=cost,
            name="sweep",
        )(whole_numbers, reals, column_sends, row_sends, pno_energy, amplitudes, integrals, column_blocks, column_margin,
          row_margin, *pieces)
        if not last:
            column_out, row_out = outs
    return (amplitudes, residual)


def solution(mesh):
    in_specs = (
        P(BOTH, None, None),
        P(BOTH, None, None),
        P(BOTH, None),
        P(BOTH),
        P(BOTH, None, None),
        P(BOTH, None, None),
        P(BOTH),
        P(BOTH),
        P(BOTH),
        P(BOTH),
        P(BOTH),
        P(BOTH),
        P(BOTH, None),
        P(BOTH, None),
        P(BOTH, None),
    )
    out_specs = (P(BOTH, None, None), P(BOTH, None, None))
    return jax.shard_map(shards, mesh=mesh, in_specs=in_specs, out_specs=out_specs, check_vma=False)
```

```python
import functools

import jax
import jax.numpy as jnp
from jax import lax
from jax.experimental import pallas as pl
from jax.experimental.pallas import tpu as pltpu
from jax.sharding import PartitionSpec as P

ITERS = 2
CHUNK = 32
BOTH = ("oi", "oj")
VMEM = pl.BlockSpec(memory_space=pltpu.VMEM)
SMEM = pl.BlockSpec(memory_space=pltpu.SMEM)
ANY = pl.BlockSpec(memory_space=pl.ANY)
HBM = pl.BlockSpec(memory_space=pltpu.HBM)
LIMIT = 50 * 1024 * 1024


def pack_rows(frozen, row_sends, row_out):
    capacity = row_sends.shape[1]
    pairs, pno, _ = frozen.shape
    for pair in range(pairs):
        row_out[pair * pno : (pair + 1) * pno, :] = frozen[pair]
    row_out[pairs * pno :, :] = jnp.zeros((row_out.shape[0] - pairs * pno, pno), row_out.dtype)
    row_out[pairs * pno :, :capacity] = row_sends[...].astype(jnp.float32).astype(row_out.dtype)


def pack_columns(column_sends, pairs, column_out):
    peers, capacity = column_sends.shape
    pno = column_out.shape[1]
    for peer in range(peers):
        for slot in range(capacity):
            row = pl.multiple_of(column_sends[peer, slot] * pno, pno)
            column_out[peer * capacity + slot] = pairs[pl.ds(row, pno), :]


def first_pack(amplitudes, row_sends, row_out, frozen):
    frozen[...] = amplitudes[...].astype(jnp.bfloat16)
    pack_rows(frozen, row_sends, row_out)


def start_margins(margin, held, sems, live):
    for chunk in range(sems.shape[0]):
        rows = pl.ds(chunk * CHUNK, CHUNK)

        @pl.when(chunk * CHUNK < live)
        def _():
            pltpu.make_async_copy(margin.at[rows], held.at[rows], sems.at[chunk]).start()


def couple(margin, held, sems, live, block, target, coupling, total):
    def one_chunk(chunk, carry):
        rows = pl.ds(chunk * CHUNK, CHUNK)
        pltpu.make_async_copy(margin.at[rows], held.at[rows], sems.at[chunk]).wait()
        terms = [chunk * CHUNK + step for step in range(CHUNK)]
        halves = [
            jnp.dot(held[term], block(term), preferred_element_type=jnp.float32).astype(jnp.bfloat16) for term in terms
        ]
        wholes = [
            lax.dot_general(half, held[term], (((1,), (1,)), ((), ())), preferred_element_type=jnp.float32)
            for half, term in zip(halves, terms)
        ]
        for whole, term in zip(wholes, terms):
            weight = jnp.where(term < live, coupling(term), 0.0)
            pair = target(term)
            total[pair] = total[pair] + weight * whole
        return carry

    lax.fori_loop(0, (live + CHUNK - 1) // CHUNK, one_chunk, 0)


def sweep_kernel(last, width, whole_numbers, reals, row_sends, energy, amplitudes, integrals, column_blocks,
                 column_margin, row_margin, *rest):
    pieces, rest = rest[:11], rest[11:]
    updated, residual = rest[:2]
    (column_held, row_held, column_sems, row_sems, blocks, stage, listed, piece_sems, list_sem, column_total, row_total,
     frozen) = rest[-12:]
    column_live, row_live, me = whole_numbers[4, 0], whole_numbers[4, 1], whole_numbers[4, 2]
    pno = energy.shape[1]
    half = pieces[7].shape[0]
    plan = [(0, 0, width, 0, 0), (1, 0, width, 7, 0), (2, 0, width, 1, 0), (3, 0, width, 6, 0), (4, 0, width, 2, 0),
            (5, 0, width, 5, 0), (6, 0, width, 3, 0), (7, 0, half, 4, 0), (8, 0, width - half, 4, half)]
    plan += [(9, i * width, width, 8 + place, 0) for i, place in enumerate((0, 7, 1, 6, 2))]
    plan += [(10, i * width, width, 8 + place, 0) for i, place in enumerate((5, 3, 4))]
    copies = [
        pltpu.make_async_copy(pieces[piece].at[pl.ds(row, rows)], blocks.at[pl.ds(place * width + there, rows)], piece_sems.at[i])
        for i, (piece, row, rows, place, there) in enumerate(plan)
    ]
    start_margins(column_margin, column_held, column_sems, column_live)
    for copy in copies:
        copy.start()
    start_margins(row_margin, row_held, row_sems, row_live)
    column_total[...] = jnp.zeros_like(column_total)
    row_total[...] = jnp.zeros_like(row_total)
    for copy in copies:
        copy.wait()
    for place in range(stage.shape[0]):
        lists = blocks[place * width + width - 16 : (place + 1) * width, :].astype(jnp.float32)
        mine = lax.broadcasted_iota(jnp.int32, lists.shape, 0) == me
        stage[place : place + 1, :] = jnp.sum(jnp.where(mine, lists, 0.0), axis=0, keepdims=True).astype(jnp.int32)
    to_scalars = pltpu.make_async_copy(stage, listed, list_sem)
    to_scalars.start()
    couple(
        column_margin, column_held, column_sems, column_live, lambda term: column_blocks[whole_numbers[0, term]],
        lambda term: whole_numbers[1, term], lambda term: reals[0, term], column_total,
    )
    to_scalars.wait()

    def block(term):
        place, slot = whole_numbers[2, term] // 2, whole_numbers[2, term] % 2
        row = place * width + listed[place, slot] * pno
        return blocks[pl.ds(pl.multiple_of(row, 16), pno), :]

    couple(
        row_margin, row_held, row_sems, row_live, block, lambda term: whole_numbers[3, term], lambda term: reals[1, term],
        row_total,
    )
    for pair in range(row_total.shape[0]):
        across = jnp.broadcast_to(energy[pair : pair + 1, :], row_total.shape[1:])
        gap = across.T + across + reals[2, pair]
        current = amplitudes[pair]
        left = integrals[pair] + gap * current + column_total[pair] + row_total[pair]
        fresh = current - left / gap
        updated[pair] = fresh
        residual[pair] = left
        if not last:
            frozen[pair] = fresh.astype(jnp.bfloat16)
    if not last:
        pack_rows(frozen, row_sends, rest[2])


def along_z(piece, step):
    chips = lax.axis_size("oj") // 2
    return lax.ppermute(piece, "oj", [(c + 2 * z, c + 2 * ((z + step) % chips)) for z in range(chips) for c in range(2)])


def swap_cores(piece):
    return lax.ppermute(piece, "oj", [(i, i ^ 1) for i in range(lax.axis_size("oj"))])


def stack_kernel(*refs):
    *pieces, out = refs
    rows = pieces[0].shape[0]
    for i, piece in enumerate(pieces):
        out[i * rows : (i + 1) * rows, :] = piece[...]


def stack(pieces):
    rows, columns = pieces[0].shape
    return pl.pallas_call(
        stack_kernel,
        out_shape=jax.ShapeDtypeStruct((len(pieces) * rows, columns), pieces[0].dtype),
        in_specs=[VMEM] * len(pieces),
        out_specs=VMEM,
        compiler_params=pltpu.CompilerParams(vmem_limit_bytes=LIMIT),
        cost_estimate=pl.CostEstimate(flops=0, bytes_accessed=4 * len(pieces) * rows * columns, transcendentals=0),
        name="stack",
    )(*pieces)


def gather_rows(own, first, half, numbers):
    up1, down1, up2, down2 = first
    near = stack([own, up1, down1, up2, down2])
    up3, down3 = along_z(up2, 1), along_z(down2, -1)
    up4, down4 = along_z(up2[:half], 2), along_z(down2[half:], -2)
    up3, down3, up4, down4, numbers = lax.optimization_barrier((up3, down3, up4, down4, numbers))
    far = jnp.concatenate([up3, down3, up4, down4])
    return [own, up1, down1, up2, down2, up3, down3, up4, down4, swap_cores(near), swap_cores(far)], numbers


def shards(
    amplitudes,
    integrals,
    pno_energy,
    pair_shift,
    column_margin,
    row_margin,
    column_coupling,
    row_coupling,
    column_target,
    row_target,
    column_source,
    row_source,
    column_sends,
    row_sends,
    term_counts,
):
    pairs, pno, _ = amplitudes.shape
    terms = column_margin.shape[0]
    peers, capacity = column_sends.shape
    chips = lax.axis_size("oj") // 2
    me = lax.axis_index("oj")
    chip, core = me // 2, me % 2

    row_peer, row_slot = row_source // capacity, row_source % capacity
    place = (row_peer // 2 - chip) % chips + chips * ((row_peer + core) % 2)
    facts = jnp.concatenate([term_counts[0], me[None].astype(jnp.int32), jnp.zeros((terms - 3,), jnp.int32)])
    whole_numbers = jnp.stack([column_source, column_target, place * 2 + row_slot, row_target, facts])
    reals = jnp.stack([column_coupling, row_coupling, jnp.pad(pair_shift, (0, terms - pairs))])

    width = pairs * pno + 16
    packed = jax.ShapeDtypeStruct((width, pno), jnp.bfloat16)
    whole = jax.ShapeDtypeStruct((pairs, pno, pno), jnp.float32)
    params = pltpu.CompilerParams(vmem_limit_bytes=LIMIT)
    margins = [pltpu.VMEM((terms, pno, pno), jnp.bfloat16)] * 2 + [pltpu.SemaphoreType.DMA((terms // CHUNK,))] * 2
    frozen = pltpu.VMEM((pairs, pno, pno), jnp.bfloat16)
    cost = pl.CostEstimate(flops=8 * terms * pno**3, bytes_accessed=4 * terms * pno**2, transcendentals=0)

    row_out = pl.pallas_call(
        first_pack,
        out_shape=packed,
        in_specs=[VMEM, VMEM],
        out_specs=VMEM,
        scratch_shapes=[frozen],
        compiler_params=params,
        name="pack_rows",
    )(amplitudes, row_sends)
    residual = integrals
    for sweep in range(ITERS):
        last = sweep == ITERS - 1
        first = [along_z(row_out, step) for step in (1, -1, 2, -2)]
        column_out = pl.pallas_call(
            pack_columns,
            out_shape=jax.ShapeDtypeStruct((peers * capacity, pno, pno), jnp.bfloat16),
            in_specs=[SMEM, VMEM],
            out_specs=VMEM,
            compiler_params=params,
            name="pack_columns",
        )(column_sends, row_out)
        if sweep:
            column_out, *first = lax.optimization_barrier((column_out, *first))
        column_blocks = lax.all_to_all(column_out, "oi", split_axis=0, concat_axis=0, tiled=True)
        pieces, (whole_numbers, reals) = gather_rows(row_out, first, pairs // 2 * pno, (whole_numbers, reals))
        amplitudes, residual, *outs = pl.pallas_call(
            functools.partial(sweep_kernel, last, width),
            out_shape=(whole, whole) + (() if last else (packed,)),
            in_specs=[SMEM] * 2 + [VMEM] * 5 + [HBM] * 2 + [ANY] * len(pieces),
            out_specs=(VMEM,) * (2 if last else 3),
            scratch_shapes=margins
            + [
                pltpu.VMEM((2 * chips * width, pno), jnp.bfloat16),
                pltpu.VMEM((2 * chips, pno), jnp.int32),
                pltpu.SMEM((2 * chips, pno), jnp.int32),
                pltpu.SemaphoreType.DMA((17,)),
                pltpu.SemaphoreType.DMA,
                pltpu.VMEM((pairs, pno, pno), jnp.float32),
                pltpu.VMEM((pairs, pno, pno), jnp.float32),
                frozen,
            ],
            compiler_params=params,
            cost_estimate=cost,
            name="sweep",
        )(whole_numbers, reals, row_sends, pno_energy, amplitudes, integrals, column_blocks, column_margin,
          row_margin, *pieces)
        if not last:
            (row_out,) = outs
    return (amplitudes, residual)


def solution(mesh):
    in_specs = (
        P(BOTH, None, None),
        P(BOTH, None, None),
        P(BOTH, None),
        P(BOTH),
        P(BOTH, None, None),
        P(BOTH, None, None),
        P(BOTH),
        P(BOTH),
        P(BOTH),
        P(BOTH),
        P(BOTH),
        P(BOTH),
        P(BOTH, None),
        P(BOTH, None),
        P(BOTH, None),
    )
    out_specs = (P(BOTH, None, None), P(BOTH, None, None))
    return jax.shard_map(shards, mesh=mesh, in_specs=in_specs, out_specs=out_specs, check_vma=False)
```

```python
import functools

import jax
import jax.numpy as jnp
from jax import lax
from jax.experimental import pallas as pl
from jax.experimental.pallas import tpu as pltpu
from jax.sharding import PartitionSpec as P

ITERS = 2
CHUNK = 32
BOTH = ("oi", "oj")
VMEM = pl.BlockSpec(memory_space=pltpu.VMEM)
SMEM = pl.BlockSpec(memory_space=pltpu.SMEM)
ANY = pl.BlockSpec(memory_space=pl.ANY)
HBM = pl.BlockSpec(memory_space=pltpu.HBM)
LIMIT = 50 * 1024 * 1024


def pack_rows(frozen, row_sends, row_out):
    capacity = row_sends.shape[1]
    pairs, pno, _ = frozen.shape
    for pair in range(pairs):
        row_out[pair * pno : (pair + 1) * pno, :] = frozen[pair]
    row_out[pairs * pno :, :] = jnp.zeros((row_out.shape[0] - pairs * pno, pno), row_out.dtype)
    row_out[pairs * pno :, :capacity] = row_sends[...].astype(jnp.float32).astype(row_out.dtype)


def pack_columns(column_sends, row_out, column_out):
    peers, capacity = column_sends.shape
    pno = column_out.shape[1]
    for peer in range(peers):
        for slot in range(capacity):
            row = pl.multiple_of(column_sends[peer, slot] * pno, pno)
            column_out[peer * capacity + slot] = row_out[pl.ds(row, pno), :]


def first_pack(amplitudes, row_sends, row_out, frozen):
    frozen[...] = amplitudes[...].astype(jnp.bfloat16)
    pack_rows(frozen, row_sends, row_out)


def start_margins(margin, held, sems, live):
    for chunk in range(sems.shape[0]):
        rows = pl.ds(chunk * CHUNK, CHUNK)

        @pl.when(chunk * CHUNK < live)
        def _():
            pltpu.make_async_copy(margin.at[rows], held.at[rows], sems.at[chunk]).start()


def couple(margin, held, sems, live, block, target, coupling, total):
    def one_chunk(chunk, carry):
        rows = pl.ds(chunk * CHUNK, CHUNK)
        pltpu.make_async_copy(margin.at[rows], held.at[rows], sems.at[chunk]).wait()
        terms = [chunk * CHUNK + step for step in range(CHUNK)]
        halves = [
            jnp.dot(held[term], block(term), preferred_element_type=jnp.float32).astype(jnp.bfloat16) for term in terms
        ]
        wholes = [
            lax.dot_general(half, held[term], (((1,), (1,)), ((), ())), preferred_element_type=jnp.float32)
            for half, term in zip(halves, terms)
        ]
        for whole, term in zip(wholes, terms):
            weight = jnp.where(term < live, coupling(term), 0.0)
            pair = target(term)
            total[pair] = total[pair] + weight * whole
        return carry

    lax.fori_loop(0, (live + CHUNK - 1) // CHUNK, one_chunk, 0)


def sweep_kernel(last, width, whole_numbers, reals, column_sends, row_sends, energy, amplitudes, integrals, column_blocks,
                 column_margin, row_margin, *rest):
    pieces, rest = rest[:11], rest[11:]
    updated, residual = rest[:2]
    (column_held, row_held, column_sems, row_sems, blocks, stage, listed, piece_sems, list_sem, column_total, row_total,
     frozen) = rest[-12:]
    column_live, row_live, me = whole_numbers[4, 0], whole_numbers[4, 1], whole_numbers[4, 2]
    pno = energy.shape[1]
    half = pieces[7].shape[0]
    plan = [(0, 0, width, 0, 0), (1, 0, width, 7, 0), (2, 0, width, 1, 0), (3, 0, width, 6, 0), (4, 0, width, 2, 0),
            (5, 0, width, 5, 0), (6, 0, width, 3, 0), (7, 0, half, 4, 0), (8, 0, width - half, 4, half)]
    plan += [(9, i * width, width, 8 + place, 0) for i, place in enumerate((0, 7, 1, 6, 2))]
    plan += [(10, i * width, width, 8 + place, 0) for i, place in enumerate((5, 3, 4))]
    copies = [
        pltpu.make_async_copy(pieces[piece].at[pl.ds(row, rows)], blocks.at[pl.ds(place * width + there, rows)], piece_sems.at[i])
        for i, (piece, row, rows, place, there) in enumerate(plan)
    ]
    start_margins(column_margin, column_held, column_sems, column_live)
    for copy in copies:
        copy.start()
    start_margins(row_margin, row_held, row_sems, row_live)
    column_total[...] = jnp.zeros_like(column_total)
    row_total[...] = jnp.zeros_like(row_total)
    for copy in copies:
        copy.wait()
    for place in range(stage.shape[0]):
        lists = blocks[place * width + width - 16 : (place + 1) * width, :].astype(jnp.float32)
        mine = lax.broadcasted_iota(jnp.int32, lists.shape, 0) == me
        stage[place : place + 1, :] = jnp.sum(jnp.where(mine, lists, 0.0), axis=0, keepdims=True).astype(jnp.int32)
    to_scalars = pltpu.make_async_copy(stage, listed, list_sem)
    to_scalars.start()
    couple(
        column_margin, column_held, column_sems, column_live, lambda term: column_blocks[whole_numbers[0, term]],
        lambda term: whole_numbers[1, term], lambda term: reals[0, term], column_total,
    )
    to_scalars.wait()

    def block(term):
        place, slot = whole_numbers[2, term] // 2, whole_numbers[2, term] % 2
        row = place * width + listed[place, slot] * pno
        return blocks[pl.ds(pl.multiple_of(row, 16), pno), :]

    couple(
        row_margin, row_held, row_sems, row_live, block, lambda term: whole_numbers[3, term], lambda term: reals[1, term],
        row_total,
    )
    for pair in range(row_total.shape[0]):
        across = jnp.broadcast_to(energy[pair : pair + 1, :], row_total.shape[1:])
        gap = across.T + across + reals[2, pair]
        current = amplitudes[pair]
        left = integrals[pair] + gap * current + column_total[pair] + row_total[pair]
        fresh = current - left / gap
        updated[pair] = fresh
        residual[pair] = left
        if not last:
            frozen[pair] = fresh.astype(jnp.bfloat16)
    if not last:
        pack_rows(frozen, row_sends, rest[2])
        pack_columns(column_sends, rest[2], rest[3])


def along_z(piece, step):
    chips = lax.axis_size("oj") // 2
    return lax.ppermute(piece, "oj", [(c + 2 * z, c + 2 * ((z + step) % chips)) for z in range(chips) for c in range(2)])


def swap_cores(piece):
    return lax.ppermute(piece, "oj", [(i, i ^ 1) for i in range(lax.axis_size("oj"))])


def stack_kernel(*refs):
    *pieces, out = refs
    rows = pieces[0].shape[0]
    for i, piece in enumerate(pieces):
        out[i * rows : (i + 1) * rows, :] = piece[...]


def stack(pieces):
    rows, columns = pieces[0].shape
    return pl.pallas_call(
        stack_kernel,
        out_shape=jax.ShapeDtypeStruct((len(pieces) * rows, columns), pieces[0].dtype),
        in_specs=[VMEM] * len(pieces),
        out_specs=VMEM,
        compiler_params=pltpu.CompilerParams(vmem_limit_bytes=LIMIT),
        cost_estimate=pl.CostEstimate(flops=0, bytes_accessed=4 * len(pieces) * rows * columns, transcendentals=0),
        name="stack",
    )(*pieces)


def gather_rows(own, first, join, half, numbers):
    up1, down1, up2, down2 = first
    near = join([own, up1, down1, up2, down2])
    up3, down3 = along_z(up2, 1), along_z(down2, -1)
    up4, down4 = along_z(up2[:half], 2), along_z(down2[half:], -2)
    up3, down3, up4, down4, numbers = lax.optimization_barrier((up3, down3, up4, down4, numbers))
    far = jnp.concatenate([up3, down3, up4, down4])
    return [own, up1, down1, up2, down2, up3, down3, up4, down4, swap_cores(near), swap_cores(far)], numbers


def shards(
    amplitudes,
    integrals,
    pno_energy,
    pair_shift,
    column_margin,
    row_margin,
    column_coupling,
    row_coupling,
    column_target,
    row_target,
    column_source,
    row_source,
    column_sends,
    row_sends,
    term_counts,
):
    pairs, pno, _ = amplitudes.shape
    terms = column_margin.shape[0]
    peers, capacity = column_sends.shape
    chips = lax.axis_size("oj") // 2
    me = lax.axis_index("oj")
    chip, core = me // 2, me % 2

    row_peer, row_slot = row_source // capacity, row_source % capacity
    place = (row_peer // 2 - chip) % chips + chips * ((row_peer + core) % 2)
    facts = jnp.concatenate([term_counts[0], me[None].astype(jnp.int32), jnp.zeros((terms - 3,), jnp.int32)])
    whole_numbers = jnp.stack([column_source, column_target, place * 2 + row_slot, row_target, facts])
    reals = jnp.stack([column_coupling, row_coupling, jnp.pad(pair_shift, (0, terms - pairs))])

    width = pairs * pno + 16
    packed = jax.ShapeDtypeStruct((width, pno), jnp.bfloat16)
    packed_columns = jax.ShapeDtypeStruct((peers * capacity, pno, pno), jnp.bfloat16)
    whole = jax.ShapeDtypeStruct((pairs, pno, pno), jnp.float32)
    params = pltpu.CompilerParams(vmem_limit_bytes=LIMIT)
    margins = [pltpu.VMEM((terms, pno, pno), jnp.bfloat16)] * 2 + [pltpu.SemaphoreType.DMA((terms // CHUNK,))] * 2
    frozen = pltpu.VMEM((pairs, pno, pno), jnp.bfloat16)
    cost = pl.CostEstimate(flops=8 * terms * pno**3, bytes_accessed=4 * terms * pno**2, transcendentals=0)

    row_out = pl.pallas_call(
        first_pack,
        out_shape=packed,
        in_specs=[VMEM, VMEM],
        out_specs=VMEM,
        scratch_shapes=[frozen],
        compiler_params=params,
        name="pack_rows",
    )(amplitudes, row_sends)
    column_out = pl.pallas_call(
        pack_columns,
        out_shape=packed_columns,
        in_specs=[SMEM, VMEM],
        out_specs=VMEM,
        compiler_params=params,
        name="pack_columns",
    )(column_sends, row_out)
    residual = integrals
    for sweep in range(ITERS):
        last = sweep == ITERS - 1
        first = [along_z(row_out, step) for step in (1, -1, 2, -2)]
        column_blocks = lax.all_to_all(column_out, "oi", split_axis=0, concat_axis=0, tiled=True)
        pieces, (whole_numbers, reals) = gather_rows(row_out, first, jnp.concatenate if sweep else stack, pairs // 2 * pno, (whole_numbers, reals))
        amplitudes, residual, *outs = pl.pallas_call(
            functools.partial(sweep_kernel, last, width),
            out_shape=(whole, whole) + (() if last else (packed, packed_columns)),
            in_specs=[SMEM] * 3 + [VMEM] * 5 + [HBM] * 2 + [ANY] * len(pieces),
            out_specs=(VMEM,) * (2 if last else 4),
            scratch_shapes=margins
            + [
                pltpu.VMEM((2 * chips * width, pno), jnp.bfloat16),
                pltpu.VMEM((2 * chips, pno), jnp.int32),
                pltpu.SMEM((2 * chips, pno), jnp.int32),
                pltpu.SemaphoreType.DMA((17,)),
                pltpu.SemaphoreType.DMA,
                pltpu.VMEM((pairs, pno, pno), jnp.float32),
                pltpu.VMEM((pairs, pno, pno), jnp.float32),
                frozen,
            ],
            compiler_params=params,
            cost_estimate=cost,
            name="sweep",
        )(whole_numbers, reals, column_sends, row_sends, pno_energy, amplitudes, integrals, column_blocks, column_margin,
          row_margin, *pieces)
        if not last:
            row_out, column_out = outs
    return (amplitudes, residual)


def solution(mesh):
    in_specs = (
        P(BOTH, None, None),
        P(BOTH, None, None),
        P(BOTH, None),
        P(BOTH),
        P(BOTH, None, None),
        P(BOTH, None, None),
        P(BOTH),
        P(BOTH),
        P(BOTH),
        P(BOTH),
        P(BOTH),
        P(BOTH),
        P(BOTH, None),
        P(BOTH, None),
        P(BOTH, None),
    )
    out_specs = (P(BOTH, None, None), P(BOTH, None, None))
    return jax.shard_map(shards, mesh=mesh, in_specs=in_specs, out_specs=out_specs, check_vma=False)
```

```python
import functools

import jax
import jax.numpy as jnp
from jax import lax
from jax.experimental import pallas as pl
from jax.experimental.pallas import tpu as pltpu
from jax.sharding import PartitionSpec as P

ITERS = 2
CHUNK = 32
BOTH = ("oi", "oj")
VMEM = pl.BlockSpec(memory_space=pltpu.VMEM)
SMEM = pl.BlockSpec(memory_space=pltpu.SMEM)
ANY = pl.BlockSpec(memory_space=pl.ANY)
HBM = pl.BlockSpec(memory_space=pltpu.HBM)
LIMIT = 50 * 1024 * 1024


def pack_rows(frozen, row_sends, row_out):
    capacity = row_sends.shape[1]
    pairs, pno, _ = frozen.shape
    for pair in range(pairs):
        row_out[pair * pno : (pair + 1) * pno, :] = frozen[pair]
    row_out[pairs * pno :, :] = jnp.zeros((row_out.shape[0] - pairs * pno, pno), row_out.dtype)
    row_out[pairs * pno :, :capacity] = row_sends[...].astype(jnp.float32).astype(row_out.dtype)


def pack_columns(column_sends, row_out, column_out):
    peers, capacity = column_sends.shape
    pno = column_out.shape[1]
    for peer in range(peers):
        for slot in range(capacity):
            row = pl.multiple_of(column_sends[peer, slot] * pno, pno)
            column_out[peer * capacity + slot] = row_out[pl.ds(row, pno), :]


def first_pack(amplitudes, row_sends, row_out, frozen):
    frozen[...] = amplitudes[...].astype(jnp.bfloat16)
    pack_rows(frozen, row_sends, row_out)


def start_margins(margin, held, sems, live):
    for chunk in range(sems.shape[0]):
        copy = pltpu.make_async_copy(margin.at[pl.ds(chunk * CHUNK, CHUNK)], held.at[pl.ds(chunk * CHUNK, CHUNK)], sems.at[chunk])
        if chunk == 0:
            copy.start()
        else:
            pl.when(chunk * CHUNK < live)(copy.start)


def couple(margin, held, sems, live, block, target, coupling, total, between=None):
    def one_chunk(chunk, carry):
        rows = pl.ds(chunk * CHUNK, CHUNK)
        pltpu.make_async_copy(margin.at[rows], held.at[rows], sems.at[chunk]).wait()
        terms = [chunk * CHUNK + step for step in range(CHUNK)]
        halves = [
            jnp.dot(held[term], block(term), preferred_element_type=jnp.float32).astype(jnp.bfloat16) for term in terms
        ]
        wholes = [
            lax.dot_general(half, held[term], (((1,), (1,)), ((), ())), preferred_element_type=jnp.float32)
            for half, term in zip(halves, terms)
        ]
        for whole, term in zip(wholes, terms):
            weight = jnp.where(term < live, coupling(term), 0.0)
            pair = target(term)
            total[pair] = total[pair] + weight * whole
        return carry

    one_chunk(0, 0)
    if between is not None:
        between()
    lax.fori_loop(1, (live + CHUNK - 1) // CHUNK, one_chunk, 0)


def sweep_kernel(last, width, whole_numbers, reals, column_sends, row_sends, energy, amplitudes, integrals, column_blocks,
                 column_margin, row_margin, *rest):
    pieces, rest = rest[:11], rest[11:]
    updated, residual = rest[:2]
    (column_held, row_held, column_sems, row_sems, blocks, stage, listed, piece_sems, list_sem, column_total, row_total,
     frozen) = rest[-12:]
    column_live, row_live, me = whole_numbers[4, 0], whole_numbers[4, 1], whole_numbers[4, 2]
    pno = energy.shape[1]
    half = pieces[7].shape[0]
    plan = [(0, 0, width, 0, 0), (1, 0, width, 7, 0), (2, 0, width, 1, 0), (3, 0, width, 6, 0), (4, 0, width, 2, 0),
            (5, 0, width, 5, 0), (6, 0, width, 3, 0), (7, 0, half, 4, 0), (8, 0, width - half, 4, half)]
    plan += [(9, i * width, width, 8 + place, 0) for i, place in enumerate((0, 7, 1, 6, 2))]
    plan += [(10, i * width, width, 8 + place, 0) for i, place in enumerate((5, 3, 4))]
    copies = [
        pltpu.make_async_copy(pieces[piece].at[pl.ds(row, rows)], blocks.at[pl.ds(place * width + there, rows)], piece_sems.at[i])
        for i, (piece, row, rows, place, there) in enumerate(plan)
    ]
    start_margins(column_margin, column_held, column_sems, column_live)
    for copy in copies:
        copy.start()
    start_margins(row_margin, row_held, row_sems, row_live)
    column_total[...] = jnp.zeros_like(column_total)
    row_total[...] = jnp.zeros_like(row_total)
    to_scalars = pltpu.make_async_copy(stage, listed, list_sem)

    def take_pieces():
        for copy in copies:
            copy.wait()
        for place in range(stage.shape[0]):
            lists = blocks[place * width + width - 16 : (place + 1) * width, :].astype(jnp.float32)
            mine = lax.broadcasted_iota(jnp.int32, lists.shape, 0) == me
            stage[place : place + 1, :] = jnp.sum(jnp.where(mine, lists, 0.0), axis=0, keepdims=True).astype(jnp.int32)
        to_scalars.start()

    couple(
        column_margin, column_held, column_sems, column_live, lambda term: column_blocks[whole_numbers[0, term]],
        lambda term: whole_numbers[1, term], lambda term: reals[0, term], column_total, take_pieces,
    )
    to_scalars.wait()

    def block(term):
        place, slot = whole_numbers[2, term] // 2, whole_numbers[2, term] % 2
        row = place * width + listed[place, slot] * pno
        return blocks[pl.ds(pl.multiple_of(row, 16), pno), :]

    couple(
        row_margin, row_held, row_sems, row_live, block, lambda term: whole_numbers[3, term], lambda term: reals[1, term],
        row_total,
    )
    for pair in range(row_total.shape[0]):
        across = jnp.broadcast_to(energy[pair : pair + 1, :], row_total.shape[1:])
        gap = across.T + across + reals[2, pair]
        current = amplitudes[pair]
        left = integrals[pair] + gap * current + column_total[pair] + row_total[pair]
        fresh = current - left / gap
        updated[pair] = fresh
        residual[pair] = left
        if not last:
            frozen[pair] = fresh.astype(jnp.bfloat16)
    if not last:
        pack_rows(frozen, row_sends, rest[2])
        pack_columns(column_sends, rest[2], rest[3])


def along_z(piece, step):
    chips = lax.axis_size("oj") // 2
    return lax.ppermute(piece, "oj", [(c + 2 * z, c + 2 * ((z + step) % chips)) for z in range(chips) for c in range(2)])


def swap_cores(piece):
    return lax.ppermute(piece, "oj", [(i, i ^ 1) for i in range(lax.axis_size("oj"))])


def stack_kernel(*refs):
    *pieces, out = refs
    rows = pieces[0].shape[0]
    for i, piece in enumerate(pieces):
        out[i * rows : (i + 1) * rows, :] = piece[...]


def stack(pieces):
    rows, columns = pieces[0].shape
    return pl.pallas_call(
        stack_kernel,
        out_shape=jax.ShapeDtypeStruct((len(pieces) * rows, columns), pieces[0].dtype),
        in_specs=[VMEM] * len(pieces),
        out_specs=VMEM,
        compiler_params=pltpu.CompilerParams(vmem_limit_bytes=LIMIT),
        cost_estimate=pl.CostEstimate(flops=0, bytes_accessed=4 * len(pieces) * rows * columns, transcendentals=0),
        name="stack",
    )(*pieces)


def gather_rows(own, first, join, half, numbers):
    up1, down1, up2, down2 = first
    near = join([own, up1, down1, up2, down2])
    up3, down3 = along_z(up2, 1), along_z(down2, -1)
    up4, down4 = along_z(up2[:half], 2), along_z(down2[half:], -2)
    up3, down3, up4, down4, numbers = lax.optimization_barrier((up3, down3, up4, down4, numbers))
    far = jnp.concatenate([up3, down3, up4, down4])
    return [own, up1, down1, up2, down2, up3, down3, up4, down4, swap_cores(near), swap_cores(far)], numbers


def shards(
    amplitudes,
    integrals,
    pno_energy,
    pair_shift,
    column_margin,
    row_margin,
    column_coupling,
    row_coupling,
    column_target,
    row_target,
    column_source,
    row_source,
    column_sends,
    row_sends,
    term_counts,
):
    pairs, pno, _ = amplitudes.shape
    terms = column_margin.shape[0]
    peers, capacity = column_sends.shape
    chips = lax.axis_size("oj") // 2
    me = lax.axis_index("oj")
    chip, core = me // 2, me % 2

    row_peer, row_slot = row_source // capacity, row_source % capacity
    place = (row_peer // 2 - chip) % chips + chips * ((row_peer + core) % 2)
    facts = jnp.concatenate([term_counts[0], me[None].astype(jnp.int32), jnp.zeros((terms - 3,), jnp.int32)])
    whole_numbers = jnp.stack([column_source, column_target, place * 2 + row_slot, row_target, facts])
    reals = jnp.stack([column_coupling, row_coupling, jnp.pad(pair_shift, (0, terms - pairs))])

    width = pairs * pno + 16
    packed = jax.ShapeDtypeStruct((width, pno), jnp.bfloat16)
    packed_columns = jax.ShapeDtypeStruct((peers * capacity, pno, pno), jnp.bfloat16)
    whole = jax.ShapeDtypeStruct((pairs, pno, pno), jnp.float32)
    params = pltpu.CompilerParams(vmem_limit_bytes=LIMIT)
    margins = [pltpu.VMEM((terms, pno, pno), jnp.bfloat16)] * 2 + [pltpu.SemaphoreType.DMA((terms // CHUNK,))] * 2
    frozen = pltpu.VMEM((pairs, pno, pno), jnp.bfloat16)
    cost = pl.CostEstimate(flops=8 * terms * pno**3, bytes_accessed=4 * terms * pno**2, transcendentals=0)

    row_out = pl.pallas_call(
        first_pack,
        out_shape=packed,
        in_specs=[VMEM, VMEM],
        out_specs=VMEM,
        scratch_shapes=[frozen],
        compiler_params=params,
        name="pack_rows",
    )(amplitudes, row_sends)
    column_out = pl.pallas_call(
        pack_columns,
        out_shape=packed_columns,
        in_specs=[SMEM, VMEM],
        out_specs=VMEM,
        compiler_params=params,
        name="pack_columns",
    )(column_sends, row_out)
    residual = integrals
    for sweep in range(ITERS):
        last = sweep == ITERS - 1
        first = [along_z(row_out, step) for step in (1, -1, 2, -2)]
        column_blocks = lax.all_to_all(column_out, "oi", split_axis=0, concat_axis=0, tiled=True)
        pieces, (whole_numbers, reals) = gather_rows(row_out, first, jnp.concatenate if sweep else stack, pairs // 2 * pno, (whole_numbers, reals))
        amplitudes, residual, *outs = pl.pallas_call(
            functools.partial(sweep_kernel, last, width),
            out_shape=(whole, whole) + (() if last else (packed, packed_columns)),
            in_specs=[SMEM] * 3 + [VMEM] * 5 + [HBM] * 2 + [ANY] * len(pieces),
            out_specs=(VMEM,) * (2 if last else 4),
            scratch_shapes=margins
            + [
                pltpu.VMEM((2 * chips * width, pno), jnp.bfloat16),
                pltpu.VMEM((2 * chips, pno), jnp.int32),
                pltpu.SMEM((2 * chips, pno), jnp.int32),
                pltpu.SemaphoreType.DMA((17,)),
                pltpu.SemaphoreType.DMA,
                pltpu.VMEM((pairs, pno, pno), jnp.float32),
                pltpu.VMEM((pairs, pno, pno), jnp.float32),
                frozen,
            ],
            compiler_params=params,
            cost_estimate=cost,
            name="sweep",
        )(whole_numbers, reals, column_sends, row_sends, pno_energy, amplitudes, integrals, column_blocks, column_margin,
          row_margin, *pieces)
        if not last:
            row_out, column_out = outs
    return (amplitudes, residual)


def solution(mesh):
    in_specs = (
        P(BOTH, None, None),
        P(BOTH, None, None),
        P(BOTH, None),
        P(BOTH),
        P(BOTH, None, None),
        P(BOTH, None, None),
        P(BOTH),
        P(BOTH),
        P(BOTH),
        P(BOTH),
        P(BOTH),
        P(BOTH),
        P(BOTH, None),
        P(BOTH, None),
        P(BOTH, None),
    )
    out_specs = (P(BOTH, None, None), P(BOTH, None, None))
    return jax.shard_map(shards, mesh=mesh, in_specs=in_specs, out_specs=out_specs, check_vma=False)
```
